32 devices in a mesh: terms: 8 (over y, x, core), rows: 4 (over z).
Axes of the slice: x: 2, y: 2, z: 4, core: 2. Of those that a mesh axis runs over, the one named last changes fastest.
Arguments:
- psi: float32 [2, 768, 768], P(None, 'rows'), may hold values from -6 to 6
- left_ops: float32 [8, 768, 768], P('terms', 'rows'), may hold values from -0.21875 to 0.21875
- right_ops: float32 [16, 768, 768], P('terms', 'rows'), may hold values from -0.09375 to 0.09375
- term_count: int32 [8], P('terms'), may hold values from 1 to 3, 12 in all
- right_slot: int32 [24], P('terms'), may hold values from 0 to 1
- sector: int32 [24], P('terms'), may hold values from 0 to 1
- sign_bit: int32 [24], P('terms'), may hold values from 0 to 1
Outputs:
- sigma: float32 [2, 768, 768], P(None, 'rows', 'terms')
The draws below stay inside these ranges and needn't reach their ends.
Inputs may be any that keep to these rules, and one draw needn't show every extreme that they name: Owner o's live terms are its first term_count[o] slots of 3; right_slot, sector and sign_bit of the other slots have no effect.
All inputs are finite; a program needn't handle non-finite values. No bound on the sum of `term_count` on one device may be relied on, other than what follows from the above.
Results may differ from the reference program's by a relative error of at most 0.0003.
Values sent between devices are 32-bit elements; how exact they have to be, the bound alone decides.
A program may use at most 64 MiB of HBM per device.

```python
import math
import jax
import jax.numpy as jnp
import numpy as np
from jax import lax

M = 768
SECTORS = 2
TERM_DEV = 3
RIGHT_DEV = 2
OWNERS = 8
TERMS = 24
RIGHTS = 16
N_TERMS = 8


def set_ends(entries, rng, least, top_value):
    shape = entries.shape
    place = [jax.random.randint(jax.random.fold_in(rng, axis), (), 0, shape[axis]) for axis in range(len(shape))]
    entries = entries.at[tuple(place)].set(least)
    longest = shape.index(max(shape))
    place[longest] = (place[longest] + 1) % shape[longest]
    return entries.at[tuple(place)].set(top_value)


def spiked(entries, own_key, source, target, blocks, factor):
    def block_of(axis_at):
        return (jnp.arange(entries.shape[axis_at]) // (entries.shape[axis_at] // blocks)).reshape((-1,) + (1,) * (entries.ndim - 1 - axis_at))

    near = jax.random.permutation(own_key, blocks)[block_of(target)]
    far = (block_of(target) + blocks // 2) % blocks
    return jnp.where((block_of(source) == near) | (block_of(source) == far), factor * entries, entries)


def block_levels(key, dims, split, low, largest):
    gain = 1.0
    for dim, shards_of in split:
        steps = jax.random.uniform(jax.random.fold_in(jax.random.fold_in(key, 6), dim), (shards_of,), jnp.float32, low / len(split), largest / len(split))
        gain = gain * jnp.repeat(jnp.exp(steps), dims[dim] // shards_of).reshape((-1,) + (1,) * (len(dims) - 1 - dim))
    return gain


def length_profile(count, total, reach, lean):
    loads = [(1 << 20) // math.isqrt(rank ** lean) + 1 for rank in range(2, count + 1)]
    spare, counts = total - reach - (count - 1), [1] * (count - 1)
    while spare > 0:
        free = [i for i in range(count - 1) if counts[i] < reach]
        pool, budget = sum([loads[i] for i in free]), spare
        for i in free:
            extra = min(reach - counts[i], max(1, budget * loads[i] // pool), spare)
            counts[i] = counts[i] + extra
            spare = spare - extra
    return np.array([reach] + counts)


def ragged(key, count, total, bound, skew):
    if count == 2:
        one = jax.random.randint(key, (), max(1, total - bound), min(bound, total - 1) + 1)
        return jnp.stack([one, total - one])
    lengths = jnp.asarray(length_profile(count, total, bound, skew), jnp.int32)
    couples = (count - 1) // 2
    source_of, sink = lengths[1:1 + 2 * couples:2], lengths[2:2 + 2 * couples:2]
    margin = jnp.minimum(source_of - 1, bound - sink)
    moved = jax.random.randint(jax.random.fold_in(key, 1), (couples,), 0, 1 << 20) % (margin + 1)
    lengths = lengths.at[1:1 + 2 * couples:2].set(source_of - moved).at[2:2 + 2 * couples:2].set(sink + moved)
    return lengths[jax.random.permutation(jax.random.fold_in(key, 2), count)]


def noise(rng, dims, width, reach, split=(), held_as=jnp.bfloat16):
    level = block_levels(rng, dims, split, -0.22, 0.18) if split else 1.0
    entries = jax.random.normal(rng, dims, jnp.float32) * width * level
    return jnp.minimum(jnp.maximum(entries, -reach), reach).astype(held_as)


def heavy_noise(stream_key, dims, scale, limit, pieces, heavy, kind=jnp.bfloat16):
    drawn = scale * jax.random.normal(stream_key, dims, jnp.float32)
    if pieces:
        drawn = drawn * block_levels(stream_key, dims, pieces, -0.22, 0.18)
    return jnp.clip(spiked(drawn, jax.random.fold_in(stream_key, 3), *heavy), -limit, limit).astype(kind)


def setup_inputs(seed: int = 0) -> dict:
    key_list = jax.random.split(jax.random.key(seed), 8)
    return {
        "psi": noise(key_list[0], (SECTORS, M, M), 1.0, 6.0, ((1, 4),), jnp.float32),
        "left_ops": noise(key_list[1], (OWNERS, M, M), M ** -0.5, 0.21875, ((0, 8), (1, 4)), jnp.float32),
        "right_ops": heavy_noise(key_list[2], (RIGHTS, M, M), (M * TERM_DEV * N_TERMS // 2) ** -0.5, 0.09375, ((0, 8), (1, 4)), (0, 1, 8, 2.0), jnp.float32),
        "term_count": ragged(key_list[3], OWNERS, N_TERMS * TERM_DEV // 2, TERM_DEV, 2).astype(jnp.int32),
        "right_slot": set_ends(jax.random.randint(key_list[4], (TERMS,), 0, RIGHT_DEV), jax.random.fold_in(key_list[4], 1), 0, RIGHT_DEV - 1).astype(jnp.int32),
        "sector": set_ends(jax.random.randint(key_list[5], (TERMS,), 0, SECTORS), jax.random.fold_in(key_list[5], 1), 0, SECTORS - 1).astype(jnp.int32),
        "sign_bit": set_ends(jax.random.randint(key_list[6], (TERMS,), 0, 2), jax.random.fold_in(key_list[6], 1), 0, 1).astype(jnp.int32),
    }


highest_mode = lax.Precision.HIGHEST


def reference(psi, left_ops, right_ops, term_count, right_slot, sector, sign_bit):
    owner_count = term_count.shape[0]
    slot_count = right_slot.shape[0] // owner_count
    rights_each = right_ops.shape[0] // owner_count
    sector_count = psi.shape[0]
    half_axis = owner_count // 2

    def one_owner(running, owner_id):
        partner = ((owner_id + half_axis) % owner_count).astype(jnp.int32)
        left_block = lax.dynamic_index_in_dim(left_ops, owner_id, 0, keepdims=False)
        right_blocks = lax.dynamic_slice_in_dim(right_ops, (partner * rights_each).astype(jnp.int32), rights_each, 0)
        first_slot = (owner_id * slot_count).astype(jnp.int32)
        slot_ids = lax.dynamic_slice_in_dim(right_slot, first_slot, slot_count, 0)
        sector_ids = lax.dynamic_slice_in_dim(sector, first_slot, slot_count, 0)
        sign_ids = lax.dynamic_slice_in_dim(sign_bit, first_slot, slot_count, 0)
        is_live = jnp.arange(slot_count, dtype=jnp.int32) < term_count[owner_id]
        term_weight = jnp.where(is_live, 2.0 * sign_ids.astype(jnp.float32) - 1.0, 0.0)
        sector_hit = (sector_ids[None, :] == jnp.arange(sector_count, dtype=jnp.int32)[:, None]).astype(jnp.float32) * term_weight[None, :]
        slot_hit = (slot_ids[:, None] == jnp.arange(rights_each, dtype=jnp.int32)[None, :]).astype(jnp.float32)
        mixing = jnp.dot(sector_hit, slot_hit, precision=highest_mode)
        combined = jnp.einsum("sr,rab->sab", mixing, right_blocks, precision=highest_mode)
        inner_rows = jnp.einsum("ab,sbc->sac", left_block, psi, precision=highest_mode)
        return running + jnp.einsum("sac,sdc->sad", inner_rows, combined, precision=highest_mode), None

    start_value = jnp.zeros(psi.shape, jnp.float32)
    summed, _ = lax.scan(one_owner, start_value, jnp.arange(owner_count, dtype=jnp.int32))
    return summed
```

```python
import functools

import jax
import jax.numpy as jnp
from jax import lax
from jax.experimental import pallas as pl
from jax.experimental.pallas import tpu as pltpu
from jax.sharding import PartitionSpec as P

highest_mode = lax.Precision.HIGHEST
MESH = pl.DeviceIdType.MESH


def passed_along(block, axis, distance):
    devices = range(lax.axis_size(axis))
    route = [((i - distance) % len(devices), i) for i in devices]
    return lax.ppermute(block, axis, route)


def term_weights(right_slot, term_count, sign_bit):
    is_live = lax.iota(jnp.int32, right_slot.shape[0]) < term_count[0]
    return jnp.where(is_live, 2.0 * sign_bit.astype(jnp.float32) - 1.0, 0.0)


def plain_device(psi, left_ops, right_ops, term_count, right_slot, sector, sign_bit):
    live_count = term_count[0]
    term_weight = term_weights(right_slot, term_count, sign_bit)
    inner_rows = jnp.einsum(
        "an,snb->sab",
        left_ops[0],
        lax.all_gather(psi, "rows", axis=1, tiled=True),
        precision=highest_mode,
    )
    half_axis = lax.axis_size("terms") // 2
    moved_right = passed_along(right_ops, "terms", half_axis)
    segment = lax.all_gather(moved_right, "rows", axis=1, tiled=True)
    summed_zero = jnp.zeros((psi.shape[0], inner_rows.shape[1], segment.shape[1]), jnp.float32)

    def one_term(index, summed):
        right_block = lax.dynamic_index_in_dim(segment, right_slot[index], 0, keepdims=False)
        source = lax.dynamic_index_in_dim(inner_rows, sector[index], 0, keepdims=False)
        product = term_weight[index] * lax.dot_general(
            source, right_block, (((1,), (1,)), ((), ())), precision=highest_mode
        )
        return summed.at[sector[index]].add(product)

    partial_value = lax.fori_loop(0, live_count, one_term, summed_zero)
    return lax.psum_scatter(partial_value, "terms", scatter_dimension=2, tiled=True)


def split16(value):
    high = value.astype(jnp.bfloat16)
    low = (value - high.astype(jnp.float32)).astype(jnp.bfloat16)
    return high, low


def dot3(a, b, dims):
    (a_high, a_low), (b_high, b_low) = a, b
    dot = functools.partial(
        lax.dot_general,
        dimension_numbers=(dims, ((), ())),
        preferred_element_type=jnp.float32,
    )
    return dot(a_high, b_high) + (dot(a_high, b_low) + dot(a_low, b_high))


def kernel(
    T, Z, CH,
    psi_ref, left_ref, right_ref, mix_ref, out_ref,
    psi_all, left_all, mix_in, y_high, y_low, part, part_in, fin,
    c_high, c_low,
    mix_s, mix_r, pz_s, pz_r, pp_s, pp_r, ly_s, lz_s, l_r, sc_s, sc_r, fin_s, fin_r,
):
    S, rows, M = psi_ref.shape
    R = right_ref.shape[0]
    H = T // Z
    sub = rows // T
    width = rows // H
    lrows = rows // CH
    t = lax.axis_index("terms")
    z = lax.axis_index("rows")
    bit_k, bit_x = lax.rem(t, 2), lax.rem(t // 2, 2)
    tk = t + 1 - 2 * bit_k
    tx = t + 2 - 4 * bit_x
    ty = lax.rem(t + 4, T)
    txy = lax.rem(tx + 4, T)

    def near(i):
        n_near = jnp.minimum(z, Z - 1 - z)
        half = (i + 1) // 2
        paired = z - half if i % 2 else z + half
        rest = jnp.where(z < Z - 1 - z, i, Z - 1 - i)
        return jnp.where(i <= 2 * n_near, paired, rest)

    def remote(src, dst, send, recv, tt, zz):
        return pltpu.make_async_remote_copy(
            src_ref=src, dst_ref=dst, send_sem=send, recv_sem=recv,
            device_id=(tt, zz), device_id_type=MESH,
        )

    def rows_of(device):
        return pl.ds(pl.multiple_of(device * sub, 8), sub)

    barrier = pltpu.get_barrier_semaphore()
    for d in range(1, T):
        pl.semaphore_signal(barrier, 1, device_id=(lax.rem(t + d, T), z), device_id_type=MESH)
    for step in (-1, 1):
        inside = (z + step >= 0) & (z + step < Z)

        @pl.when(inside)
        def _():
            pl.semaphore_signal(barrier, 1, device_id=(t, z + step), device_id_type=MESH)

    source_plane = t // H
    own_final = source_plane == z
    for e in range(T):
        @pl.when(jnp.logical_not(own_final & (t == e)))
        def _():
            pl.semaphore_signal(barrier, 1, device_id=(jnp.int32(e), source_plane), device_id_type=MESH)

    greeted = 2 * T - 1 + jnp.where(z > 0, 1, 0) + jnp.where(z < Z - 1, 1, 0)
    pl.semaphore_wait(barrier, greeted - jnp.where(own_final, 1, 0))

    def psi_own(step):
        return remote(
            psi_ref.at[:, rows_of(t), :], psi_all.at[z, :, rows_of(t), :],
            pz_s.at[(step + 1) // 2, z], pz_r.at[z], t, z + step,
        )

    def psi_pass(zs, step):
        view = psi_all.at[zs, :, rows_of(t), :]
        return remote(view, view, pz_s.at[(step + 1) // 2, zs], pz_r.at[zs], t, z + step)

    def spread(zs, kind, piece, target):
        view = psi_all.at[zs, :, rows_of(piece), :]
        return remote(view, view, pp_s.at[zs, kind], pp_r.at[zs, kind], target, z)

    def spread_copies(zs):
        return [
            spread(zs, 0, t, ty), spread(zs, 1, t, tx), spread(zs, 2, ty, tx),
            spread(zs, 3, t, tk), spread(zs, 4, ty, tk), spread(zs, 5, tx, tk),
            spread(zs, 6, txy, tk),
        ]

    def left_first(c):
        part_rows = pl.ds(c * lrows, lrows)
        return remote(
            left_ref.at[part_rows, :], left_all.at[z, part_rows, :],
            ly_s.at[c], l_r.at[z, c], ty, z,
        )

    def left_pass(zs, c, step):
        view = left_all.at[zs, pl.ds(c * lrows, lrows), :]
        return remote(view, view, lz_s.at[(step + 1) // 2, zs, c], l_r.at[zs, c], t, z + step)

    def can_pass(zs, step):
        if step == 1:
            return (zs <= z) & (z < Z - 1)
        return (zs >= z) & (z > 0)

    def scatter(zs, d):
        peer = lax.rem(t + d, T)
        return remote(
            part.at[zs, rows_of(peer), :], part_in.at[zs, d - 1],
            sc_s.at[zs, d - 1], sc_r.at[zs, d - 1], peer, z,
        )

    def final(zs, h):
        return remote(
            fin.at[zs, h], out_ref.at[:, rows_of(t), :],
            fin_s.at[zs, h], fin_r.at[t], z * H + h, zs,
        )

    def fill_y(zs, source, s):
        value = dot3(split16(source), (c_high[s], c_low[s]), ((1,), (1,)))
        high, low = split16(value)
        y_high[s, pl.ds(pl.multiple_of(zs * rows, 16), rows), :] = high
        y_low[s, pl.ds(pl.multiple_of(zs * rows, 16), rows), :] = low

    def left_arrives(zs):
        for c in range(CH):
            left_pass(zs, c, 1).wait_recv()
            for step in (-1, 1):
                @pl.when(can_pass(zs, step))
                def _():
                    left_pass(zs, c, step).start()

    def product(zs):
        left_pair = split16(left_all[zs])
        for s in range(S):
            part[zs, :, pl.ds(s * rows, rows) if rows % 128 == 0 else slice(s * rows, (s + 1) * rows)] = dot3(
                left_pair, (y_high[s], y_low[s]), ((1,), (0,))
            )
        for d in range(1, T):
            scatter(zs, d).start()

    def finish(zs):
        for d in range(1, T):
            scatter(zs, d).wait_recv()
        total = part[zs, rows_of(t), :]
        for d in range(1, T):
            total = total + part_in[zs, d - 1]
        for s in range(S):
            for h in range(H):
                first = s * rows + h * width
                fin[zs, h, s] = total[:, first:first + width]
        for h in range(H):
            mine = (z * H + h == t) & (zs == z)

            @pl.when(mine)
            def _():
                out_ref[:, rows_of(t), :] = fin[zs, h]

            @pl.when(jnp.logical_not(mine))
            def _():
                final(zs, h).start()

    mix_copy = remote(mix_ref, mix_in, mix_s.at[0], mix_r.at[0], ty, z)
    mix_copy.start()
    for step in (-1, 1):
        @pl.when((z + step >= 0) & (z + step < Z))
        def _():
            psi_own(step).start()
    for c in range(CH):
        left_first(c).start()

    mix_copy.wait_recv()
    for s in range(S):
        total = mix_in[s * R, 0:1, 0:1] * right_ref[0]
        for r in range(1, R):
            total = total + mix_in[s * R + r, 0:1, 0:1] * right_ref[r]
        high, low = split16(total)
        c_high[s] = high
        c_low[s] = low

    for i in range(1, Z):
        zs = near(i)
        psi_pass(zs, 1).wait_recv()
        for step in (-1, 1):
            @pl.when(can_pass(zs, step))
            def _():
                psi_pass(zs, step).start()
        copies = spread_copies(zs)
        copies[0].start()
        copies[1].start()
        copies[3].start()

    for s in range(S):
        fill_y(z, psi_ref[s], s)

    def spread_on(zs):
        copies = spread_copies(zs)
        copies[0].wait_recv()
        copies[2].start()
        copies[4].start()
        copies[1].wait_recv()
        copies[5].start()
        copies[2].wait_recv()
        copies[6].start()

    def y_block(zs):
        copies = spread_copies(zs)
        for kind in range(3, 7):
            copies[kind].wait_recv()
        for s in range(S):
            fill_y(zs, psi_all[zs, s], s)

    left_arrives(near(0))
    for i in range(1, Z):
        spread_on(near(i))
        if i >= 2:
            y_block(near(i - 1))
            if i < Z - 1:
                left_arrives(near(i - 1))
    y_block(near(Z - 1))
    product(near(0))
    for i in range(1, Z):
        if i >= Z - 2 or i == 0:
            left_arrives(near(i))
        product(near(i))
        finish(near(i - 1))
    finish(near(Z - 1))

    for e in range(T):
        @pl.when(jnp.logical_not(own_final & (t == e)))
        def _():
            remote(
                fin.at[0, 0], out_ref.at[:, pl.ds(e * sub, sub), :],
                fin_s.at[0, 0], fin_r.at[e], t, z,
            ).wait_recv()

    mix_copy.wait_send()
    for c in range(CH):
        left_first(c).wait_send()
    for zs in range(Z):
        for step in (-1, 1):
            @pl.when(can_pass(zs, step))
            def _():
                psi_pass(zs, step).wait_send()
                for c in range(CH):
                    left_pass(zs, c, step).wait_send()

        @pl.when(zs != z)
        def _():
            for copy in spread_copies(zs):
                copy.wait_send()

        for d in range(1, T):
            scatter(zs, d).wait_send()
        for h in range(H):
            @pl.when(jnp.logical_not((z * H + h == t) & (zs == z)))
            def _():
                final(zs, h).wait_send()


def fused_device(T, Z, psi, left_ops, right_ops, term_count, right_slot, sector, sign_bit):
    S, rows, M = psi.shape
    R = right_ops.shape[0]
    H = T // Z
    sub = rows // T
    CH = 2
    weight = term_weights(right_slot, term_count, sign_bit)
    sector_hit = sector[None, :] == jnp.arange(S, dtype=jnp.int32)[:, None]
    slot_hit = right_slot[None, :] == jnp.arange(R, dtype=jnp.int32)[:, None]
    both = sector_hit[:, None, :] & slot_hit[None, :, :]
    mix = jnp.sum(jnp.where(both, weight, 0.0), axis=-1)
    mix = jnp.broadcast_to(mix.reshape(S * R, 1, 1), (S * R, 8, 128))
    dma = pltpu.SemaphoreType.DMA
    f32, b16 = jnp.float32, jnp.bfloat16
    vmem = pl.BlockSpec(memory_space=pltpu.VMEM)
    return pl.pallas_call(
        functools.partial(kernel, T, Z, CH),
        out_shape=jax.ShapeDtypeStruct((S, rows, rows // H), f32),
        in_specs=[vmem] * 4,
        out_specs=vmem,
        scratch_shapes=[
            pltpu.VMEM((Z, S, rows, M), f32),
            pltpu.VMEM((Z, rows, M), f32),
            pltpu.VMEM((S * R, 8, 128), f32),
            pltpu.VMEM((S, Z * rows, rows), b16),
            pltpu.VMEM((S, Z * rows, rows), b16),
            pltpu.VMEM((Z, rows, S * rows), f32),
            pltpu.VMEM((Z, T - 1, sub, S * rows), f32),
            pltpu.VMEM((Z, H, S, sub, rows // H), f32),
            pltpu.VMEM((S, rows, M), b16),
            pltpu.VMEM((S, rows, M), b16),
            dma((1,)), dma((1,)),
            dma((2, Z)), dma((Z,)),
            dma((Z, 7)), dma((Z, 7)),
            dma((CH,)), dma((2, Z, CH)), dma((Z, CH)),
            dma((Z, T - 1)), dma((Z, T - 1)),
            dma((Z, H)), dma((T,)),
        ],
        compiler_params=pltpu.CompilerParams(
            collective_id=0, has_side_effects=True, vmem_limit_bytes=40 * 1024 * 1024
        ),
        cost_estimate=pl.CostEstimate(
            flops=4 * S * M * M * rows, bytes_accessed=4 * 6 * rows * M, transcendentals=0
        ),
    )(psi, left_ops[0], right_ops, mix)


def solution(mesh):
    T, Z = mesh.shape["terms"], mesh.shape["rows"]

    def per_device(psi, left_ops, right_ops, *terms):
        M = psi.shape[2]
        rows = psi.shape[1]
        fits = (
            T == 8 and Z >= 4 and T % Z == 0 and M == Z * rows and M % 128 == 0
            and rows % (8 * T) == 0 and rows % 32 == 0 and left_ops.shape[0] == 1
        )
        if fits:
            return fused_device(T, Z, psi, left_ops, right_ops, *terms)
        return plain_device(psi, left_ops, right_ops, *terms)

    return jax.shard_map(
        per_device,
        mesh=mesh,
        in_specs=(
            P(None, "rows", None),
            P("terms", "rows", None),
            P("terms", "rows", None),
            P("terms"),
            P("terms"),
            P("terms"),
            P("terms"),
        ),
        out_specs=P(None, "rows", "terms"),
        check_vma=False,
    )
```

```python
import functools

import jax
import jax.numpy as jnp
from jax import lax
from jax.experimental import pallas as pl
from jax.experimental.pallas import tpu as pltpu
from jax.sharding import PartitionSpec as P

highest_mode = lax.Precision.HIGHEST
MESH = pl.DeviceIdType.MESH


def passed_along(block, axis, distance):
    devices = range(lax.axis_size(axis))
    route = [((i - distance) % len(devices), i) for i in devices]
    return lax.ppermute(block, axis, route)


def term_weights(right_slot, term_count, sign_bit):
    is_live = lax.iota(jnp.int32, right_slot.shape[0]) < term_count[0]
    return jnp.where(is_live, 2.0 * sign_bit.astype(jnp.float32) - 1.0, 0.0)


def plain_device(psi, left_ops, right_ops, term_count, right_slot, sector, sign_bit):
    live_count = term_count[0]
    term_weight = term_weights(right_slot, term_count, sign_bit)
    inner_rows = jnp.einsum(
        "an,snb->sab",
        left_ops[0],
        lax.all_gather(psi, "rows", axis=1, tiled=True),
        precision=highest_mode,
    )
    half_axis = lax.axis_size("terms") // 2
    moved_right = passed_along(right_ops, "terms", half_axis)
    segment = lax.all_gather(moved_right, "rows", axis=1, tiled=True)
    summed_zero = jnp.zeros((psi.shape[0], inner_rows.shape[1], segment.shape[1]), jnp.float32)

    def one_term(index, summed):
        right_block = lax.dynamic_index_in_dim(segment, right_slot[index], 0, keepdims=False)
        source = lax.dynamic_index_in_dim(inner_rows, sector[index], 0, keepdims=False)
        product = term_weight[index] * lax.dot_general(
            source, right_block, (((1,), (1,)), ((), ())), precision=highest_mode
        )
        return summed.at[sector[index]].add(product)

    partial_value = lax.fori_loop(0, live_count, one_term, summed_zero)
    return lax.psum_scatter(partial_value, "terms", scatter_dimension=2, tiled=True)


def split16(value):
    high = value.astype(jnp.bfloat16)
    low = (value - high.astype(jnp.float32)).astype(jnp.bfloat16)
    return high, low


def dot3(a, b, dims):
    (a_high, a_low), (b_high, b_low) = a, b
    dot = functools.partial(
        lax.dot_general,
        dimension_numbers=(dims, ((), ())),
        preferred_element_type=jnp.float32,
    )
    return dot(a_high, b_high) + (dot(a_high, b_low) + dot(a_low, b_high))


def kernel(
    T, Z, CH,
    psi_ref, left_ref, right_ref, mix_ref, out_ref,
    psi_all, left_all, mix_in, y_high, y_low, part, part_in, fin,
    c_high, c_low,
    right_in, local_s,
    mix_s, mix_r, pz_s, pz_r, pp_s, pp_r, ly_s, lz_s, l_r, sc_s, sc_r, fin_s, fin_r,
):
    S, rows, M = psi_ref.shape
    R = right_ref.shape[0]
    H = T // Z
    sub = rows // T
    width = rows // H
    lrows = rows // CH
    t = lax.axis_index("terms")
    z = lax.axis_index("rows")
    bit_k, bit_x = lax.rem(t, 2), lax.rem(t // 2, 2)
    tk = t + 1 - 2 * bit_k
    tx = t + 2 - 4 * bit_x
    ty = lax.rem(t + 4, T)
    txy = lax.rem(tx + 4, T)

    def near(i):
        n_near = jnp.minimum(z, Z - 1 - z)
        half = (i + 1) // 2
        paired = z - half if i % 2 else z + half
        rest = jnp.where(z < Z - 1 - z, i, Z - 1 - i)
        return jnp.where(i <= 2 * n_near, paired, rest)

    def remote(src, dst, send, recv, tt, zz):
        return pltpu.make_async_remote_copy(
            src_ref=src, dst_ref=dst, send_sem=send, recv_sem=recv,
            device_id=(tt, zz), device_id_type=MESH,
        )

    def rows_of(device):
        return pl.ds(pl.multiple_of(device * sub, 8), sub)

    psi_copy = pltpu.make_async_copy(psi_ref, psi_all.at[z], local_s.at[0])
    right_copy = pltpu.make_async_copy(right_ref, right_in, local_s.at[1])
    psi_copy.start()
    right_copy.start()

    barrier = pltpu.get_barrier_semaphore()
    for d in range(1, T):
        pl.semaphore_signal(barrier, 1, device_id=(lax.rem(t + d, T), z), device_id_type=MESH)
    for step in (-1, 1):
        inside = (z + step >= 0) & (z + step < Z)

        @pl.when(inside)
        def _():
            pl.semaphore_signal(barrier, 1, device_id=(t, z + step), device_id_type=MESH)

    source_plane = t // H
    own_final = source_plane == z
    for e in range(T):
        @pl.when(jnp.logical_not(own_final & (t == e)))
        def _():
            pl.semaphore_signal(barrier, 1, device_id=(jnp.int32(e), source_plane), device_id_type=MESH)

    greeted = 2 * T - 1 + jnp.where(z > 0, 1, 0) + jnp.where(z < Z - 1, 1, 0)
    pl.semaphore_wait(barrier, greeted - jnp.where(own_final, 1, 0))

    def psi_own(step):
        return remote(
            psi_ref.at[:, rows_of(t), :], psi_all.at[z, :, rows_of(t), :],
            pz_s.at[(step + 1) // 2, z], pz_r.at[z], t, z + step,
        )

    def psi_pass(zs, step):
        view = psi_all.at[zs, :, rows_of(t), :]
        return remote(view, view, pz_s.at[(step + 1) // 2, zs], pz_r.at[zs], t, z + step)

    def spread(zs, kind, piece, target):
        view = psi_all.at[zs, :, rows_of(piece), :]
        return remote(view, view, pp_s.at[zs, kind], pp_r.at[zs, kind], target, z)

    def spread_copies(zs):
        return [
            spread(zs, 0, t, ty), spread(zs, 1, t, tx), spread(zs, 2, ty, tx),
            spread(zs, 3, t, tk), spread(zs, 4, ty, tk), spread(zs, 5, tx, tk),
            spread(zs, 6, txy, tk),
        ]

    def left_first(c):
        part_rows = pl.ds(c * lrows, lrows)
        return remote(
            left_ref.at[part_rows, :], left_all.at[z, part_rows, :],
            ly_s.at[c], l_r.at[z, c], ty, z,
        )

    def left_pass(zs, c, step):
        view = left_all.at[zs, pl.ds(c * lrows, lrows), :]
        return remote(view, view, lz_s.at[(step + 1) // 2, zs, c], l_r.at[zs, c], t, z + step)

    def can_pass(zs, step):
        if step == 1:
            return (zs <= z) & (z < Z - 1)
        return (zs >= z) & (z > 0)

    def scatter(zs, d):
        peer = lax.rem(t + d, T)
        return remote(
            part.at[zs, rows_of(peer), :], part_in.at[zs, d - 1],
            sc_s.at[zs, d - 1], sc_r.at[zs, d - 1], peer, z,
        )

    def final(zs, h):
        return remote(
            fin.at[zs, h], out_ref.at[:, rows_of(t), :],
            fin_s.at[zs, h], fin_r.at[t], z * H + h, zs,
        )

    def fill_y(zs, source, s):
        value = dot3(split16(source), (c_high[s], c_low[s]), ((1,), (1,)))
        high, low = split16(value)
        y_high[s, pl.ds(pl.multiple_of(zs * rows, 16), rows), :] = high
        y_low[s, pl.ds(pl.multiple_of(zs * rows, 16), rows), :] = low

    def left_arrives(zs):
        for c in range(CH):
            left_pass(zs, c, 1).wait_recv()
            for step in (-1, 1):
                @pl.when(can_pass(zs, step))
                def _():
                    left_pass(zs, c, step).start()

    def product(zs):
        left_pair = split16(left_all[zs])
        for s in range(S):
            part[zs, :, pl.ds(s * rows, rows) if rows % 128 == 0 else slice(s * rows, (s + 1) * rows)] = dot3(
                left_pair, (y_high[s], y_low[s]), ((1,), (0,))
            )
        for d in range(1, T):
            scatter(zs, d).start()

    def finish(zs):
        for d in range(1, T):
            scatter(zs, d).wait_recv()
        total = part[zs, rows_of(t), :]
        for d in range(1, T):
            total = total + part_in[zs, d - 1]
        for s in range(S):
            for h in range(H):
                first = s * rows + h * width
                fin[zs, h, s] = total[:, first:first + width]
        for h in range(H):
            mine = (z * H + h == t) & (zs == z)

            @pl.when(mine)
            def _():
                out_ref[:, rows_of(t), :] = fin[zs, h]

            @pl.when(jnp.logical_not(mine))
            def _():
                final(zs, h).start()

    mix_copy = remote(mix_ref, mix_in, mix_s.at[0], mix_r.at[0], ty, z)
    mix_copy.start()
    for step in (-1, 1):
        @pl.when((z + step >= 0) & (z + step < Z))
        def _():
            psi_own(step).start()
    for c in range(CH):
        left_first(c).start()

    right_copy.wait()
    mix_copy.wait_recv()
    for s in range(S):
        total = mix_in[s * R, 0:1, 0:1] * right_in[0]
        for r in range(1, R):
            total = total + mix_in[s * R + r, 0:1, 0:1] * right_in[r]
        high, low = split16(total)
        c_high[s] = high
        c_low[s] = low

    def psi_arrives(zs):
        psi_pass(zs, 1).wait_recv()
        for step in (-1, 1):
            @pl.when(can_pass(zs, step))
            def _():
                psi_pass(zs, step).start()
        spread(zs, 0, t, ty).start()
        spread(zs, 1, t, tx).start()
        spread(zs, 3, t, tk).start()

    for i in range(1, Z - 1):
        psi_arrives(near(i))
    left_arrives(near(0))
    psi_arrives(near(Z - 1))

    psi_copy.wait()
    for s in range(S):
        fill_y(z, psi_all[z, s], s)

    def spread_on(zs):
        copies = spread_copies(zs)
        copies[0].wait_recv()
        copies[2].start()
        copies[4].start()
        copies[1].wait_recv()
        copies[5].start()
        copies[2].wait_recv()
        copies[6].start()

    def y_block(zs):
        copies = spread_copies(zs)
        for kind in range(3, 7):
            copies[kind].wait_recv()
        for s in range(S):
            fill_y(zs, psi_all[zs, s], s)

    for i in range(1, Z):
        spread_on(near(i))
        if i >= 2:
            y_block(near(i - 1))
            if i < Z - 1:
                left_arrives(near(i - 1))
    y_block(near(Z - 1))
    product(near(0))
    for i in range(1, Z):
        if i >= Z - 2 or i == 0:
            left_arrives(near(i))
        product(near(i))
        finish(near(i - 1))
    finish(near(Z - 1))

    for e in range(T):
        @pl.when(jnp.logical_not(own_final & (t == e)))
        def _():
            remote(
                fin.at[0, 0], out_ref.at[:, pl.ds(e * sub, sub), :],
                fin_s.at[0, 0], fin_r.at[e], t, z,
            ).wait_recv()

    mix_copy.wait_send()
    for c in range(CH):
        left_first(c).wait_send()
    for zs in range(Z):
        for step in (-1, 1):
            @pl.when(can_pass(zs, step))
            def _():
                psi_pass(zs, step).wait_send()
                for c in range(CH):
                    left_pass(zs, c, step).wait_send()

        @pl.when(zs != z)
        def _():
            for copy in spread_copies(zs):
                copy.wait_send()

        for d in range(1, T):
            scatter(zs, d).wait_send()
        for h in range(H):
            @pl.when(jnp.logical_not((z * H + h == t) & (zs == z)))
            def _():
                final(zs, h).wait_send()


def fused_device(T, Z, psi, left_ops, right_ops, term_count, right_slot, sector, sign_bit):
    S, rows, M = psi.shape
    R = right_ops.shape[0]
    H = T // Z
    sub = rows // T
    CH = 2
    weight = term_weights(right_slot, term_count, sign_bit)
    sector_hit = sector[None, :] == jnp.arange(S, dtype=jnp.int32)[:, None]
    slot_hit = right_slot[None, :] == jnp.arange(R, dtype=jnp.int32)[:, None]
    both = sector_hit[:, None, :] & slot_hit[None, :, :]
    mix = jnp.sum(jnp.where(both, weight, 0.0), axis=-1)
    mix = jnp.broadcast_to(mix.reshape(S * R, 1, 1), (S * R, 8, 128))
    dma = pltpu.SemaphoreType.DMA
    f32, b16 = jnp.float32, jnp.bfloat16
    anyw = pl.BlockSpec(memory_space=pl.ANY)
    vmem = pl.BlockSpec(memory_space=pltpu.VMEM)
    return pl.pallas_call(
        functools.partial(kernel, T, Z, CH),
        out_shape=jax.ShapeDtypeStruct((S, rows, rows // H), f32),
        in_specs=[anyw] * 3 + [vmem],
        out_specs=vmem,
        scratch_shapes=[
            pltpu.VMEM((Z, S, rows, M), f32),
            pltpu.VMEM((Z, rows, M), f32),
            pltpu.VMEM((S * R, 8, 128), f32),
            pltpu.VMEM((S, Z * rows, rows), b16),
            pltpu.VMEM((S, Z * rows, rows), b16),
            pltpu.VMEM((Z, rows, S * rows), f32),
            pltpu.VMEM((Z, T - 1, sub, S * rows), f32),
            pltpu.VMEM((Z, H, S, sub, rows // H), f32),
            pltpu.VMEM((S, rows, M), b16),
            pltpu.VMEM((S, rows, M), b16),
            pltpu.VMEM((R, rows, M), f32), dma((2,)),
            dma((1,)), dma((1,)),
            dma((2, Z)), dma((Z,)),
            dma((Z, 7)), dma((Z, 7)),
            dma((CH,)), dma((2, Z, CH)), dma((Z, CH)),
            dma((Z, T - 1)), dma((Z, T - 1)),
            dma((Z, H)), dma((T,)),
        ],
        compiler_params=pltpu.CompilerParams(
            collective_id=0, has_side_effects=True, vmem_limit_bytes=40 * 1024 * 1024
        ),
        cost_estimate=pl.CostEstimate(
            flops=4 * S * M * M * rows, bytes_accessed=4 * 6 * rows * M, transcendentals=0
        ),
    )(psi, left_ops[0], right_ops, mix)


def solution(mesh):
    T, Z = mesh.shape["terms"], mesh.shape["rows"]

    def per_device(psi, left_ops, right_ops, *terms):
        M = psi.shape[2]
        rows = psi.shape[1]
        fits = (
            T == 8 and Z >= 4 and T % Z == 0 and M == Z * rows and M % 128 == 0
            and rows % (8 * T) == 0 and rows % 32 == 0 and left_ops.shape[0] == 1
        )
        if fits:
            return fused_device(T, Z, psi, left_ops, right_ops, *terms)
        return plain_device(psi, left_ops, right_ops, *terms)

    return jax.shard_map(
        per_device,
        mesh=mesh,
        in_specs=(
            P(None, "rows", None),
            P("terms", "rows", None),
            P("terms", "rows", None),
            P("terms"),
            P("terms"),
            P("terms"),
            P("terms"),
        ),
        out_specs=P(None, "rows", "terms"),
        check_vma=False,
    )
```

```python
import functools

import jax
import jax.numpy as jnp
from jax import lax
from jax.experimental import pallas as pl
from jax.experimental.pallas import tpu as pltpu
from jax.sharding import PartitionSpec as P

highest_mode = lax.Precision.HIGHEST
MESH = pl.DeviceIdType.MESH


def passed_along(block, axis, distance):
    devices = range(lax.axis_size(axis))
    route = [((i - distance) % len(devices), i) for i in devices]
    return lax.ppermute(block, axis, route)


def term_weights(right_slot, term_count, sign_bit):
    is_live = lax.iota(jnp.int32, right_slot.shape[0]) < term_count[0]
    return jnp.where(is_live, 2.0 * sign_bit.astype(jnp.float32) - 1.0, 0.0)


def plain_device(psi, left_ops, right_ops, term_count, right_slot, sector, sign_bit):
    live_count = term_count[0]
    term_weight = term_weights(right_slot, term_count, sign_bit)
    inner_rows = jnp.einsum(
        "an,snb->sab",
        left_ops[0],
        lax.all_gather(psi, "rows", axis=1, tiled=True),
        precision=highest_mode,
    )
    half_axis = lax.axis_size("terms") // 2
    moved_right = passed_along(right_ops, "terms", half_axis)
    segment = lax.all_gather(moved_right, "rows", axis=1, tiled=True)
    summed_zero = jnp.zeros((psi.shape[0], inner_rows.shape[1], segment.shape[1]), jnp.float32)

    def one_term(index, summed):
        right_block = lax.dynamic_index_in_dim(segment, right_slot[index], 0, keepdims=False)
        source = lax.dynamic_index_in_dim(inner_rows, sector[index], 0, keepdims=False)
        product = term_weight[index] * lax.dot_general(
            source, right_block, (((1,), (1,)), ((), ())), precision=highest_mode
        )
        return summed.at[sector[index]].add(product)

    partial_value = lax.fori_loop(0, live_count, one_term, summed_zero)
    return lax.psum_scatter(partial_value, "terms", scatter_dimension=2, tiled=True)


def split16(value):
    high = value.astype(jnp.bfloat16)
    low = (value - high.astype(jnp.float32)).astype(jnp.bfloat16)
    return high, low


def dot3(a, b, dims):
    (a_high, a_low), (b_high, b_low) = a, b
    dot = functools.partial(
        lax.dot_general,
        dimension_numbers=(dims, ((), ())),
        preferred_element_type=jnp.float32,
    )
    return dot(a_high, b_high) + (dot(a_high, b_low) + dot(a_low, b_high))


def kernel(
    T, Z, CH,
    psi_ref, left_ref, right_ref, mix_ref, out_ref,
    psi_all, left_all, mix_in, y_high, y_low, part, part_in, fin,
    c_high, c_low,
    right_in, local_s,
    mix_s, mix_r, pz_s, pz_r, pp_s, pp_r, ly_s, lz_s, l_r, sc_s, sc_r, fin_s, fin_r,
):
    S, rows, M = psi_ref.shape
    R = right_ref.shape[0]
    H = T // Z
    sub = rows // T
    width = rows // H
    lrows = rows // CH
    t = lax.axis_index("terms")
    z = lax.axis_index("rows")
    bit_k, bit_x = lax.rem(t, 2), lax.rem(t // 2, 2)
    tk = t + 1 - 2 * bit_k
    tx = t + 2 - 4 * bit_x
    ty = lax.rem(t + 4, T)
    txy = lax.rem(tx + 4, T)

    def near(i):
        n_near = jnp.minimum(z, Z - 1 - z)
        half = (i + 1) // 2
        paired = z - half if i % 2 else z + half
        rest = jnp.where(z < Z - 1 - z, i, Z - 1 - i)
        return jnp.where(i <= 2 * n_near, paired, rest)

    def remote(src, dst, send, recv, tt, zz):
        return pltpu.make_async_remote_copy(
            src_ref=src, dst_ref=dst, send_sem=send, recv_sem=recv,
            device_id=(tt, zz), device_id_type=MESH,
        )

    def rows_of(device):
        return pl.ds(pl.multiple_of(device * sub, 8), sub)

    psi_copy = pltpu.make_async_copy(psi_ref, psi_all.at[z], local_s.at[0])
    right_copy = pltpu.make_async_copy(right_ref, right_in, local_s.at[1])
    psi_copy.start()
    right_copy.start()

    barrier = pltpu.get_barrier_semaphore()
    for d in range(1, T):
        pl.semaphore_signal(barrier, 1, device_id=(lax.rem(t + d, T), z), device_id_type=MESH)
    for step in (-1, 1):
        inside = (z + step >= 0) & (z + step < Z)

        @pl.when(inside)
        def _():
            pl.semaphore_signal(barrier, 1, device_id=(t, z + step), device_id_type=MESH)

    source_plane = t // H
    own_final = source_plane == z
    for e in range(T):
        @pl.when(jnp.logical_not(own_final & (t == e)))
        def _():
            pl.semaphore_signal(barrier, 1, device_id=(jnp.int32(e), source_plane), device_id_type=MESH)

    greeted = 2 * T - 1 + jnp.where(z > 0, 1, 0) + jnp.where(z < Z - 1, 1, 0)
    pl.semaphore_wait(barrier, greeted - jnp.where(own_final, 1, 0))

    def psi_own(step):
        return remote(
            psi_ref.at[:, rows_of(t), :], psi_all.at[z, :, rows_of(t), :],
            pz_s.at[(step + 1) // 2, z], pz_r.at[z], t, z + step,
        )

    def psi_pass(zs, step):
        view = psi_all.at[zs, :, rows_of(t), :]
        return remote(view, view, pz_s.at[(step + 1) // 2, zs], pz_r.at[zs], t, z + step)

    def spread(zs, kind, piece, target):
        view = psi_all.at[zs, :, rows_of(piece), :]
        return remote(view, view, pp_s.at[zs, kind], pp_r.at[zs, kind], target, z)

    def spread_copies(zs):
        return [
            spread(zs, 0, t, ty), spread(zs, 1, t, tx), spread(zs, 2, ty, tx),
            spread(zs, 3, t, tk), spread(zs, 4, ty, tk), spread(zs, 5, tx, tk),
            spread(zs, 6, txy, tk),
        ]

    def left_first(c):
        part_rows = pl.ds(c * lrows, lrows)
        return remote(
            left_ref.at[part_rows, :], left_all.at[z, part_rows, :],
            ly_s.at[c], l_r.at[z, c], ty, z,
        )

    def left_pass(zs, c, step):
        view = left_all.at[zs, pl.ds(c * lrows, lrows), :]
        return remote(view, view, lz_s.at[(step + 1) // 2, zs, c], l_r.at[zs, c], t, z + step)

    def can_pass(zs, step):
        if step == 1:
            return (zs <= z) & (z < Z - 1)
        return (zs >= z) & (z > 0)

    def scatter(zs, d):
        peer = lax.rem(t + d, T)
        return remote(
            part.at[zs, rows_of(peer), :], part_in.at[zs, d - 1],
            sc_s.at[zs, d - 1], sc_r.at[zs, d - 1], peer, z,
        )

    def final(zs, h):
        return remote(
            fin.at[zs, h], out_ref.at[:, rows_of(t), :],
            fin_s.at[zs, h], fin_r.at[t], z * H + h, zs,
        )

    def fill_y(zs, source, s):
        value = dot3(split16(source), (c_high[s], c_low[s]), ((1,), (1,)))
        high, low = split16(value)
        y_high[s, pl.ds(pl.multiple_of(zs * rows, 16), rows), :] = high
        y_low[s, pl.ds(pl.multiple_of(zs * rows, 16), rows), :] = low

    is_end = (z == 0) | (z == Z - 1)

    def left_arrives(zs, chunks=range(CH)):
        for c in chunks:
            left_pass(zs, c, 1).wait_recv()
            for step in (-1, 1):
                @pl.when(can_pass(zs, step))
                def _():
                    left_pass(zs, c, step).start()

    def inner_takes(zs):
        @pl.when(jnp.logical_not(is_end))
        def _():
            left_arrives(zs)

    def end_takes(zs):
        @pl.when(is_end)
        def _():
            for c in range(CH):
                left_pass(zs, c, 1).wait_recv()

    def product(zs):
        left_pair = split16(left_all[zs])
        for s in range(S):
            part[zs, :, pl.ds(s * rows, rows) if rows % 128 == 0 else slice(s * rows, (s + 1) * rows)] = dot3(
                left_pair, (y_high[s], y_low[s]), ((1,), (0,))
            )
        for d in range(1, T):
            scatter(zs, d).start()

    def finish(zs):
        for d in range(1, T):
            scatter(zs, d).wait_recv()
        total = part[zs, rows_of(t), :]
        for d in range(1, T):
            total = total + part_in[zs, d - 1]
        for s in range(S):
            for h in range(H):
                first = s * rows + h * width
                fin[zs, h, s] = total[:, first:first + width]
        for h in range(H):
            mine = (z * H + h == t) & (zs == z)

            @pl.when(mine)
            def _():
                out_ref[:, rows_of(t), :] = fin[zs, h]

            @pl.when(jnp.logical_not(mine))
            def _():
                final(zs, h).start()

    mix_copy = remote(mix_ref, mix_in, mix_s.at[0], mix_r.at[0], ty, z)
    mix_copy.start()
    for step in (-1, 1):
        @pl.when((z + step >= 0) & (z + step < Z))
        def _():
            psi_own(step).start()
    for c in range(CH):
        left_first(c).start()

    def psi_arrives(zs):
        psi_pass(zs, 1).wait_recv()
        for step in (-1, 1):
            @pl.when(can_pass(zs, step))
            def _():
                psi_pass(zs, step).start()
        spread(zs, 0, t, ty).start()
        spread(zs, 1, t, tx).start()
        spread(zs, 3, t, tk).start()

    psi_arrives(near(1))
    right_copy.wait()
    mix_copy.wait_recv()
    for s in range(S):
        total = mix_in[s * R, 0:1, 0:1] * right_in[0]
        for r in range(1, R):
            total = total + mix_in[s * R + r, 0:1, 0:1] * right_in[r]
        high, low = split16(total)
        c_high[s] = high
        c_low[s] = low
    left_arrives(near(0), range(CH // 2))
    for i in range(2, Z - 1):
        psi_arrives(near(i))
    left_arrives(near(0), range(CH // 2, CH))
    psi_arrives(near(Z - 1))

    psi_copy.wait()
    for s in range(S):
        fill_y(z, psi_all[z, s], s)

    def spread_on(zs):
        copies = spread_copies(zs)
        copies[0].wait_recv()
        copies[2].start()
        copies[4].start()
        copies[1].wait_recv()
        copies[5].start()
        copies[2].wait_recv()
        copies[6].start()

    def y_block(zs):
        copies = spread_copies(zs)
        for kind in range(3, 7):
            copies[kind].wait_recv()
        for s in range(S):
            fill_y(zs, psi_all[zs, s], s)

    spread_on(near(1))
    spread_on(near(2))
    inner_takes(near(1))
    for i in range(3, Z):
        spread_on(near(i))
    y_block(near(1))
    inner_takes(near(2))
    for i in range(2, Z):
        y_block(near(i))
    product(near(0))
    end_takes(near(1))
    product(near(1))
    for i in range(3, Z):
        inner_takes(near(i))
    finish(near(0))
    for i in range(2, Z):
        end_takes(near(i))
        product(near(i))
        finish(near(i - 1))
    finish(near(Z - 1))

    for e in range(T):
        @pl.when(jnp.logical_not(own_final & (t == e)))
        def _():
            remote(
                fin.at[0, 0], out_ref.at[:, pl.ds(e * sub, sub), :],
                fin_s.at[0, 0], fin_r.at[e], t, z,
            ).wait_recv()

    mix_copy.wait_send()
    for c in range(CH):
        left_first(c).wait_send()
    for zs in range(Z):
        for step in (-1, 1):
            @pl.when(can_pass(zs, step))
            def _():
                psi_pass(zs, step).wait_send()
                for c in range(CH):
                    left_pass(zs, c, step).wait_send()

        @pl.when(zs != z)
        def _():
            for copy in spread_copies(zs):
                copy.wait_send()

        for d in range(1, T):
            scatter(zs, d).wait_send()
        for h in range(H):
            @pl.when(jnp.logical_not((z * H + h == t) & (zs == z)))
            def _():
                final(zs, h).wait_send()


def fused_device(T, Z, psi, left_ops, right_ops, term_count, right_slot, sector, sign_bit):
    S, rows, M = psi.shape
    R = right_ops.shape[0]
    H = T // Z
    sub = rows // T
    CH = 4
    weight = term_weights(right_slot, term_count, sign_bit)
    sector_hit = sector[None, :] == jnp.arange(S, dtype=jnp.int32)[:, None]
    slot_hit = right_slot[None, :] == jnp.arange(R, dtype=jnp.int32)[:, None]
    both = sector_hit[:, None, :] & slot_hit[None, :, :]
    mix = jnp.sum(jnp.where(both, weight, 0.0), axis=-1)
    mix = jnp.broadcast_to(mix.reshape(S * R, 1, 1), (S * R, 8, 128))
    dma = pltpu.SemaphoreType.DMA
    f32, b16 = jnp.float32, jnp.bfloat16
    anyw = pl.BlockSpec(memory_space=pl.ANY)
    vmem = pl.BlockSpec(memory_space=pltpu.VMEM)
    return pl.pallas_call(
        functools.partial(kernel, T, Z, CH),
        out_shape=jax.ShapeDtypeStruct((S, rows, rows // H), f32),
        in_specs=[anyw] * 3 + [vmem],
        out_specs=vmem,
        scratch_shapes=[
            pltpu.VMEM((Z, S, rows, M), f32),
            pltpu.VMEM((Z, rows, M), f32),
            pltpu.VMEM((S * R, 8, 128), f32),
            pltpu.VMEM((S, Z * rows, rows), b16),
            pltpu.VMEM((S, Z * rows, rows), b16),
            pltpu.VMEM((Z, rows, S * rows), f32),
            pltpu.VMEM((Z, T - 1, sub, S * rows), f32),
            pltpu.VMEM((Z, H, S, sub, rows // H), f32),
            pltpu.VMEM((S, rows, M), b16),
            pltpu.VMEM((S, rows, M), b16),
            pltpu.VMEM((R, rows, M), f32), dma((2,)),
            dma((1,)), dma((1,)),
            dma((2, Z)), dma((Z,)),
            dma((Z, 7)), dma((Z, 7)),
            dma((CH,)), dma((2, Z, CH)), dma((Z, CH)),
            dma((Z, T - 1)), dma((Z, T - 1)),
            dma((Z, H)), dma((T,)),
        ],
        compiler_params=pltpu.CompilerParams(
            collective_id=0, has_side_effects=True, vmem_limit_bytes=40 * 1024 * 1024
        ),
        cost_estimate=pl.CostEstimate(
            flops=4 * S * M * M * rows, bytes_accessed=4 * 6 * rows * M, transcendentals=0
        ),
    )(psi, left_ops[0], right_ops, mix)


def solution(mesh):
    T, Z = mesh.shape["terms"], mesh.shape["rows"]

    def per_device(psi, left_ops, right_ops, *terms):
        M = psi.shape[2]
        rows = psi.shape[1]
        fits = (
            T == 8 and Z >= 4 and T % Z == 0 and M == Z * rows and M % 128 == 0
            and rows % (8 * T) == 0 and rows % 32 == 0 and left_ops.shape[0] == 1
        )
        if fits:
            return fused_device(T, Z, psi, left_ops, right_ops, *terms)
        return plain_device(psi, left_ops, right_ops, *terms)

    return jax.shard_map(
        per_device,
        mesh=mesh,
        in_specs=(
            P(None, "rows", None),
            P("terms", "rows", None),
            P("terms", "rows", None),
            P("terms"),
            P("terms"),
            P("terms"),
            P("terms"),
        ),
        out_specs=P(None, "rows", "terms"),
        check_vma=False,
    )
```

```python
import functools

import jax
import jax.numpy as jnp
from jax import lax
from jax.experimental import pallas as pl
from jax.experimental.pallas import tpu as pltpu
from jax.sharding import PartitionSpec as P

highest_mode = lax.Precision.HIGHEST
MESH = pl.DeviceIdType.MESH


def passed_along(block, axis, distance):
    devices = range(lax.axis_size(axis))
    route = [((i - distance) % len(devices), i) for i in devices]
    return lax.ppermute(block, axis, route)


def term_weights(right_slot, term_count, sign_bit):
    is_live = lax.iota(jnp.int32, right_slot.shape[0]) < term_count[0]
    return jnp.where(is_live, 2.0 * sign_bit.astype(jnp.float32) - 1.0, 0.0)


def plain_device(psi, left_ops, right_ops, term_count, right_slot, sector, sign_bit):
    live_count = term_count[0]
    term_weight = term_weights(right_slot, term_count, sign_bit)
    inner_rows = jnp.einsum(
        "an,snb->sab",
        left_ops[0],
        lax.all_gather(psi, "rows", axis=1, tiled=True),
        precision=highest_mode,
    )
    half_axis = lax.axis_size("terms") // 2
    moved_right = passed_along(right_ops, "terms", half_axis)
    segment = lax.all_gather(moved_right, "rows", axis=1, tiled=True)
    summed_zero = jnp.zeros((psi.shape[0], inner_rows.shape[1], segment.shape[1]), jnp.float32)

    def one_term(index, summed):
        right_block = lax.dynamic_index_in_dim(segment, right_slot[index], 0, keepdims=False)
        source = lax.dynamic_index_in_dim(inner_rows, sector[index], 0, keepdims=False)
        product = term_weight[index] * lax.dot_general(
            source, right_block, (((1,), (1,)), ((), ())), precision=highest_mode
        )
        return summed.at[sector[index]].add(product)

    partial_value = lax.fori_loop(0, live_count, one_term, summed_zero)
    return lax.psum_scatter(partial_value, "terms", scatter_dimension=2, tiled=True)


def split16(value):
    high = value.astype(jnp.bfloat16)
    low = (value - high.astype(jnp.float32)).astype(jnp.bfloat16)
    return high, low


def dot3(a, b, dims):
    (a_high, a_low), (b_high, b_low) = a, b
    dot = functools.partial(
        lax.dot_general,
        dimension_numbers=(dims, ((), ())),
        preferred_element_type=jnp.float32,
    )
    return dot(a_high, b_high) + (dot(a_high, b_low) + dot(a_low, b_high))


def kernel(
    T, Z, CH,
    psi_ref, left_ref, right_ref, mix_ref, out_ref,
    psi_all, left_all, mix_in, y_high, y_low, part, part_in, fin,
    c_high, c_low,
    right_in, local_s,
    mix_s, mix_r, pz_s, pz_r, pp_s, pp_r, ly_s, lz_s, l_r, sc_s, sc_r, fin_s, fin_r,
):
    S, rows, M = psi_ref.shape
    R = right_ref.shape[0]
    H = T // Z
    sub = rows // T
    width = rows // H
    lrows = rows // CH
    t = lax.axis_index("terms")
    z = lax.axis_index("rows")
    bit_k, bit_x = lax.rem(t, 2), lax.rem(t // 2, 2)
    tk = t + 1 - 2 * bit_k
    tx = t + 2 - 4 * bit_x
    ty = lax.rem(t + 4, T)
    txy = lax.rem(tx + 4, T)

    def near(i):
        n_near = jnp.minimum(z, Z - 1 - z)
        half = (i + 1) // 2
        paired = z - half if i % 2 else z + half
        rest = jnp.where(z < Z - 1 - z, i, Z - 1 - i)
        return jnp.where(i <= 2 * n_near, paired, rest)

    def remote(src, dst, send, recv, tt, zz):
        return pltpu.make_async_remote_copy(
            src_ref=src, dst_ref=dst, send_sem=send, recv_sem=recv,
            device_id=(tt, zz), device_id_type=MESH,
        )

    def rows_of(device):
        return pl.ds(pl.multiple_of(device * sub, 8), sub)

    psi_copy = pltpu.make_async_copy(psi_ref, psi_all.at[z], local_s.at[0])
    right_copy = pltpu.make_async_copy(right_ref, right_in, local_s.at[1])
    psi_copy.start()
    right_copy.start()

    barrier = pltpu.get_barrier_semaphore()
    for d in range(1, T):
        pl.semaphore_signal(barrier, 1, device_id=(lax.rem(t + d, T), z), device_id_type=MESH)
    for step in (-1, 1):
        inside = (z + step >= 0) & (z + step < Z)

        @pl.when(inside)
        def _():
            pl.semaphore_signal(barrier, 1, device_id=(t, z + step), device_id_type=MESH)

    source_plane = t // H
    own_final = source_plane == z
    for e in range(T):
        @pl.when(jnp.logical_not(own_final & (t == e)))
        def _():
            pl.semaphore_signal(barrier, 1, device_id=(jnp.int32(e), source_plane), device_id_type=MESH)

    greeted = 2 * T - 1 + jnp.where(z > 0, 1, 0) + jnp.where(z < Z - 1, 1, 0)
    pl.semaphore_wait(barrier, greeted - jnp.where(own_final, 1, 0))

    def psi_own(step):
        return remote(
            psi_ref.at[:, rows_of(t), :], psi_all.at[z, :, rows_of(t), :],
            pz_s.at[(step + 1) // 2, z], pz_r.at[z], t, z + step,
        )

    def psi_pass(zs, step):
        view = psi_all.at[zs, :, rows_of(t), :]
        return remote(view, view, pz_s.at[(step + 1) // 2, zs], pz_r.at[zs], t, z + step)

    def spread(zs, kind, piece, target):
        view = psi_all.at[zs, :, rows_of(piece), :]
        return remote(view, view, pp_s.at[zs, kind], pp_r.at[zs, kind], target, z)

    def spread_copies(zs):
        return [
            spread(zs, 0, t, ty), spread(zs, 1, t, tx), spread(zs, 2, ty, tx),
            spread(zs, 3, t, tk), spread(zs, 4, ty, tk), spread(zs, 5, tx, tk),
            spread(zs, 6, txy, tk),
        ]

    def left_first(c):
        part_rows = pl.ds(c * lrows, lrows)
        return remote(
            left_ref.at[part_rows, :], left_all.at[z, part_rows, :],
            ly_s.at[c], l_r.at[z, c], ty, z,
        )

    def left_pass(zs, c, step):
        view = left_all.at[zs, pl.ds(c * lrows, lrows), :]
        return remote(view, view, lz_s.at[(step + 1) // 2, zs, c], l_r.at[zs, c], t, z + step)

    def can_pass(zs, step):
        if step == 1:
            return (zs <= z) & (z < Z - 1)
        return (zs >= z) & (z > 0)

    def scatter(zs, d):
        peer = lax.rem(t + d, T)
        return remote(
            part.at[zs, rows_of(peer), :], part_in.at[zs, d - 1],
            sc_s.at[zs, d - 1], sc_r.at[zs, d - 1], peer, z,
        )

    def final(zs, h):
        return remote(
            fin.at[zs, h], out_ref.at[:, rows_of(t), :],
            fin_s.at[zs, h], fin_r.at[t], z * H + h, zs,
        )

    def fill_y(zs, source, s):
        value = dot3(split16(source), (c_high[s], c_low[s]), ((1,), (1,)))
        high, low = split16(value)
        y_high[s, pl.ds(pl.multiple_of(zs * rows, 16), rows), :] = high
        y_low[s, pl.ds(pl.multiple_of(zs * rows, 16), rows), :] = low

    is_end = (z == 0) | (z == Z - 1)

    def left_arrives(zs, chunks=range(CH)):
        for c in chunks:
            left_pass(zs, c, 1).wait_recv()
            for step in (-1, 1):
                @pl.when(can_pass(zs, step))
                def _():
                    left_pass(zs, c, step).start()

    def inner_takes(zs):
        @pl.when(jnp.logical_not(is_end))
        def _():
            left_arrives(zs)

    def end_takes(zs):
        @pl.when(is_end)
        def _():
            for c in range(CH):
                left_pass(zs, c, 1).wait_recv()

    def product(zs):
        left_pair = split16(left_all[zs])
        for s in range(S):
            part[zs, :, pl.ds(s * rows, rows) if rows % 128 == 0 else slice(s * rows, (s + 1) * rows)] = dot3(
                left_pair, (y_high[s], y_low[s]), ((1,), (0,))
            )
        for d in range(1, T):
            scatter(zs, d).start()

    def finish(zs):
        for d in range(1, T):
            scatter(zs, d).wait_recv()
        total = part[zs, rows_of(t), :]
        for d in range(1, T):
            total = total + part_in[zs, d - 1]
        for s in range(S):
            for h in range(H):
                first = s * rows + h * width
                fin[zs, h, s] = total[:, first:first + width]
        for h in range(H):
            mine = (z * H + h == t) & (zs == z)

            @pl.when(mine)
            def _():
                out_ref[:, rows_of(t), :] = fin[zs, h]

            @pl.when(jnp.logical_not(mine))
            def _():
                final(zs, h).start()

    mix_copy = remote(mix_ref, mix_in, mix_s.at[0], mix_r.at[0], ty, z)
    mix_copy.start()
    for step in (-1, 1):
        @pl.when((z + step >= 0) & (z + step < Z))
        def _():
            psi_own(step).start()
    for c in range(CH):
        left_first(c).start()

    def psi_arrives(zs):
        psi_pass(zs, 1).wait_recv()
        for step in (-1, 1):
            @pl.when(can_pass(zs, step))
            def _():
                psi_pass(zs, step).start()
        spread(zs, 0, t, ty).start()
        spread(zs, 1, t, tx).start()
        spread(zs, 3, t, tk).start()

    psi_arrives(near(1))
    right_copy.wait()
    mix_copy.wait_recv()
    for s in range(S):
        total = mix_in[s * R, 0:1, 0:1] * right_in[0]
        for r in range(1, R):
            total = total + mix_in[s * R + r, 0:1, 0:1] * right_in[r]
        high, low = split16(total)
        c_high[s] = high
        c_low[s] = low
    left_arrives(near(0), range(CH // 2))
    for i in range(2, Z - 1):
        psi_arrives(near(i))
    left_arrives(near(0), range(CH // 2, CH))
    psi_arrives(near(Z - 1))

    psi_copy.wait()
    for s in range(S):
        fill_y(z, psi_all[z, s], s)

    def spread_on(zs):
        copies = spread_copies(zs)
        copies[0].wait_recv()
        copies[2].start()
        copies[4].start()
        copies[1].wait_recv()
        copies[5].start()
        copies[2].wait_recv()
        copies[6].start()

    def y_block(zs):
        copies = spread_copies(zs)
        for kind in range(3, 7):
            copies[kind].wait_recv()
        for s in range(S):
            fill_y(zs, psi_all[zs, s], s)

    spread_on(near(1))
    spread_on(near(2))
    inner_takes(near(1))
    inner_takes(near(2))
    for i in range(3, Z):
        spread_on(near(i))
    for i in range(1, Z):
        y_block(near(i))
    product(near(0))
    end_takes(near(1))
    product(near(1))
    for i in range(3, Z):
        inner_takes(near(i))
    finish(near(0))
    for i in range(2, Z):
        end_takes(near(i))
        product(near(i))
        finish(near(i - 1))
    finish(near(Z - 1))

    for e in range(T):
        @pl.when(jnp.logical_not(own_final & (t == e)))
        def _():
            remote(
                fin.at[0, 0], out_ref.at[:, pl.ds(e * sub, sub), :],
                fin_s.at[0, 0], fin_r.at[e], t, z,
            ).wait_recv()

    mix_copy.wait_send()
    for c in range(CH):
        left_first(c).wait_send()
    for zs in range(Z):
        for step in (-1, 1):
            @pl.when(can_pass(zs, step))
            def _():
                psi_pass(zs, step).wait_send()
                for c in range(CH):
                    left_pass(zs, c, step).wait_send()

        @pl.when(zs != z)
        def _():
            for copy in spread_copies(zs):
                copy.wait_send()

        for d in range(1, T):
            scatter(zs, d).wait_send()
        for h in range(H):
            @pl.when(jnp.logical_not((z * H + h == t) & (zs == z)))
            def _():
                final(zs, h).wait_send()


def fused_device(T, Z, psi, left_ops, right_ops, term_count, right_slot, sector, sign_bit):
    S, rows, M = psi.shape
    R = right_ops.shape[0]
    H = T // Z
    sub = rows // T
    CH = 4
    weight = term_weights(right_slot, term_count, sign_bit)
    sector_hit = sector[None, :] == jnp.arange(S, dtype=jnp.int32)[:, None]
    slot_hit = right_slot[None, :] == jnp.arange(R, dtype=jnp.int32)[:, None]
    both = sector_hit[:, None, :] & slot_hit[None, :, :]
    mix = jnp.sum(jnp.where(both, weight, 0.0), axis=-1)
    mix = jnp.broadcast_to(mix.reshape(S * R, 1, 1), (S * R, 8, 128))
    dma = pltpu.SemaphoreType.DMA
    f32, b16 = jnp.float32, jnp.bfloat16
    anyw = pl.BlockSpec(memory_space=pl.ANY)
    vmem = pl.BlockSpec(memory_space=pltpu.VMEM)
    return pl.pallas_call(
        functools.partial(kernel, T, Z, CH),
        out_shape=jax.ShapeDtypeStruct((S, rows, rows // H), f32),
        in_specs=[anyw] * 3 + [vmem],
        out_specs=vmem,
        scratch_shapes=[
            pltpu.VMEM((Z, S, rows, M), f32),
            pltpu.VMEM((Z, rows, M), f32),
            pltpu.VMEM((S * R, 8, 128), f32),
            pltpu.VMEM((S, Z * rows, rows), b16),
            pltpu.VMEM((S, Z * rows, rows), b16),
            pltpu.VMEM((Z, rows, S * rows), f32),
            pltpu.VMEM((Z, T - 1, sub, S * rows), f32),
            pltpu.VMEM((Z, H, S, sub, rows // H), f32),
            pltpu.VMEM((S, rows, M), b16),
            pltpu.VMEM((S, rows, M), b16),
            pltpu.VMEM((R, rows, M), f32), dma((2,)),
            dma((1,)), dma((1,)),
            dma((2, Z)), dma((Z,)),
            dma((Z, 7)), dma((Z, 7)),
            dma((CH,)), dma((2, Z, CH)), dma((Z, CH)),
            dma((Z, T - 1)), dma((Z, T - 1)),
            dma((Z, H)), dma((T,)),
        ],
        compiler_params=pltpu.CompilerParams(
            collective_id=0, has_side_effects=True, vmem_limit_bytes=40 * 1024 * 1024
        ),
        cost_estimate=pl.CostEstimate(
            flops=4 * S * M * M * rows, bytes_accessed=4 * 6 * rows * M, transcendentals=0
        ),
    )(psi, left_ops[0], right_ops, mix)


def solution(mesh):
    T, Z = mesh.shape["terms"], mesh.shape["rows"]

    def per_device(psi, left_ops, right_ops, *terms):
        M = psi.shape[2]
        rows = psi.shape[1]
        fits = (
            T == 8 and Z >= 4 and T % Z == 0 and M == Z * rows and M % 128 == 0
            and rows % (8 * T) == 0 and rows % 32 == 0 and left_ops.shape[0] == 1
        )
        if fits:
            return fused_device(T, Z, psi, left_ops, right_ops, *terms)
        return plain_device(psi, left_ops, right_ops, *terms)

    return jax.shard_map(
        per_device,
        mesh=mesh,
        in_specs=(
            P(None, "rows", None),
            P("terms", "rows", None),
            P("terms", "rows", None),
            P("terms"),
            P("terms"),
            P("terms"),
            P("terms"),
        ),
        out_specs=P(None, "rows", "terms"),
        check_vma=False,
    )
```
